32 devices in a mesh: scene: 2 (over y), pulse: 4 (over z), range: 2 (over x), rep: 2 (over core).
Axes of the slice: x: 2, y: 2, z: 4, core: 2. Of those that a mesh axis runs over, the one named last changes fastest.
Arguments:
- echo: bfloat16 [8, 64, 2, 6144], P(('scene', 'pulse'), 'rep', None, 'range'), parts along dimension 0, may hold values from -6 to 6
- chirp: bfloat16 [2, 512], replicated, may hold values from -0.1875 to 0.1875
- beam_one: int32 [2, 128], replicated, may hold values from 0 to 63, as said below
- shift_one: int32 [2, 128], replicated, may hold values from -28 to 28
- frac_one: float32 [2, 128], replicated, may hold values from 0 to 1
- base_one: float32 [2, 128], replicated, may hold values from -3.140625 to 3.140625
- beam_two: int32 [2, 256], replicated, may hold values from 0 to 127, as said below
- shift_two: int32 [2, 256], replicated, may hold values from -28 to 28
- frac_two: float32 [2, 256], replicated, may hold values from 0 to 1
- base_two: float32 [2, 256], replicated, may hold values from -3.140625 to 3.140625
Outputs:
- image: bfloat16 [2, 8, 32, 2, 6144], P('rep', ('scene', 'pulse'), None, None, 'range'), parts along dimension 1
The draws below stay inside these ranges and needn't reach their ends.
There are 2 independent parts, one for each index of `scene`. The reference program is written for one: setup_inputs(seed, part) draws one part's arguments, and reference() takes and returns one part's arrays. A program takes and returns all parts, laid end to end along the dimension named above; an argument that names none is the same for every part. Nothing has to cross between parts.
Inputs may be any that keep to these rules, and one draw needn't show every extreme that they name: beam_one[c, p] differs from p // 2 by at most 1 and lies in the same aligned block of 8 child beams as p // 2; the first and last parent beams read child beams 0 and 63. beam_two[c, p] differs from p // 2 by at most 1 and lies in the same aligned block of 16 child beams as p // 2; the first and last parent beams read child beams 0 and 127.
All inputs are finite; a program needn't handle non-finite values.
Results may differ from the reference program's by a relative error of at most 0.012.
Values may be sent and summed in bfloat16 or wider, within the bound.
A program may use at most 64 MiB of HBM per device.

```python
import jax
import jax.numpy as jnp
from jax import lax

BD = 32
CH = 512
OMAX = 28
HALO = 32
SUBS = 4
B0 = 64
B1 = 128
B2 = 256
RANGE = 6144
N_PULSE = 4
N_REP = 2


def child_table(key, parent_count, half_count):
    parents = jnp.arange(parent_count).astype(jnp.int32)
    centre = parents // 2
    lowest = centre // half_count * half_count
    offsets = jax.random.randint(key, (2, parent_count), -1, 2).astype(jnp.int32)
    edges = (parents == 0) | (parents == parent_count - 1)
    offsets = jnp.where(edges[None, :], 0, offsets)
    return jnp.clip(centre[None, :] + offsets, lowest[None, :], lowest[None, :] + half_count - 1).astype(jnp.int32)


def draw_beam_one(key, part):
    return child_table(jax.random.fold_in(key, 11), B1, BD // 4)


def draw_beam_two(key, part):
    return child_table(jax.random.fold_in(key, 23), B2, BD // 2)


def touch_ends(values, stream_key, least, top_value):
    index_at = [jax.random.randint(jax.random.fold_in(stream_key, axis), (), 0, length) for axis, length in enumerate(values.shape)]
    main_axis = values.shape.index(max(values.shape))
    beside = index_at[:main_axis] + [(index_at[main_axis] + 1) % values.shape[main_axis]] + index_at[main_axis + 1:]
    return values.at[tuple(index_at)].set(least).at[tuple(beside)].set(top_value)


def block_scale(own_key, dims, shards, smallest, high):
    factor_of = 1.0
    for position, blocks in shards:
        heights = jax.random.uniform(jax.random.fold_in(jax.random.fold_in(own_key, 6), position), (blocks,), jnp.float32, smallest / len(shards), high / len(shards))
        factor_of = factor_of * jnp.repeat(jnp.exp(heights), dims[position] // blocks).reshape((-1,) + (1,) * (len(dims) - 1 - position))
    return factor_of


def bell_draw(own_key, extent, scale, reach, shards=(), dtype=jnp.bfloat16):
    factor_of = block_scale(own_key, extent, shards, -0.22, 0.18) if shards else 1.0
    entries = jax.random.normal(own_key, extent, jnp.float32) * scale * factor_of
    return jnp.minimum(jnp.maximum(entries, -reach), reach).astype(dtype)


def setup_inputs(seed: int = 0, part: int = 0) -> dict:
    streams_of = jax.random.split(jax.random.key(seed), 11)
    own_keys = jax.random.split(jax.random.fold_in(streams_of[10], part), 11)
    return {
        "echo": bell_draw(own_keys[0], (SUBS, B0, 2, RANGE), 1.0, 6.0, ((0, 4), (1, 2), (3, 2))),
        "chirp": bell_draw(streams_of[1], (2, CH), (2 * CH) ** -0.5, 0.1875),
        "beam_one": draw_beam_one(jax.random.fold_in(streams_of[10], 71), part),
        "shift_one": touch_ends(jax.random.randint(streams_of[3], (2, B1), 0 - OMAX, OMAX + 1), jax.random.fold_in(streams_of[3], 1), 0 - OMAX, OMAX).astype(jnp.int32),
        "frac_one": jnp.clip(jax.random.uniform(streams_of[4], (2, B1), jnp.float32, 0.0, 1.0), 0.0, 1.0),
        "base_one": jnp.clip(jax.random.uniform(streams_of[5], (2, B1), jnp.float32, -3.140625, 3.140625), -3.140625, 3.140625),
        "beam_two": draw_beam_two(jax.random.fold_in(streams_of[10], 71), part),
        "shift_two": touch_ends(jax.random.randint(streams_of[7], (2, B2), 0 - OMAX, OMAX + 1), jax.random.fold_in(streams_of[7], 1), 0 - OMAX, OMAX).astype(jnp.int32),
        "frac_two": jnp.clip(jax.random.uniform(streams_of[8], (2, B2), jnp.float32, 0.0, 1.0), 0.0, 1.0),
        "base_two": jnp.clip(jax.random.uniform(streams_of[9], (2, B2), jnp.float32, -3.140625, 3.140625), -3.140625, 3.140625),
    }


def correlate_all(echo, chirp):
    real_part = chirp[0].astype(jnp.float32)
    imag_part = chirp[1].astype(jnp.float32)
    kernel = jnp.stack([jnp.stack([real_part, imag_part]), jnp.stack([-imag_part, real_part])])

    def one_subaperture(subimage):
        signal = subimage.astype(jnp.float32)
        result = lax.conv_general_dilated(signal, kernel, (1,), [(0, CH - 1)], dimension_numbers=("NCH", "OIH", "NCH"), precision=lax.Precision.HIGHEST)
        return result.astype(jnp.bfloat16)

    return lax.map(one_subaperture, echo)


def tap_table(frac_table):
    spread = (jnp.arange(8).astype(jnp.float32) - 3.0)[None, None, :] - frac_table[..., None]
    return jnp.sinc(spread) * (0.54 + 0.46 * jnp.cos(jnp.pi * spread / 4.0))


def merge_level(images, beam_table, shift_table, frac_table, base_table):
    pair_count = images.shape[0] // 2
    parent_count = beam_table.shape[1]
    bin_total = images.shape[3]
    tap_weights = tap_table(frac_table)
    range_ramp = jnp.arange(bin_total).astype(jnp.float32) / bin_total - 0.5
    seg_len = bin_total + 7

    def slide(line_data, offset_start):
        return lax.dynamic_slice_in_dim(line_data, offset_start, seg_len, 1)

    def one_pair(pair_index):
        merged = jnp.zeros((parent_count, 2, bin_total), jnp.float32)
        for child in range(2):
            child_image = lax.dynamic_index_in_dim(images, 2 * pair_index + child, 0, keepdims=False)
            chosen = jnp.take(child_image, beam_table[child], axis=0)
            padded = jnp.pad(chosen, ((0, 0), (0, 0), (HALO, HALO)))
            starts = (HALO - 3 + shift_table[child]).astype(jnp.int32)
            segments = jax.vmap(slide)(padded, starts)
            interpolated = jnp.zeros((parent_count, 2, bin_total), jnp.float32)
            for tap_index in range(8):
                interpolated = interpolated + tap_weights[child, :, tap_index, None, None] * segments[:, :, tap_index:tap_index + bin_total].astype(jnp.float32)
            phase_angle = base_table[child][:, None] + 0.5 * (shift_table[child].astype(jnp.float32) + frac_table[child])[:, None] * range_ramp[None, :]
            cosine = jnp.cos(phase_angle)
            sine_part = jnp.sin(phase_angle)
            rotated = jnp.stack([interpolated[:, 0] * cosine - interpolated[:, 1] * sine_part, interpolated[:, 0] * sine_part + interpolated[:, 1] * cosine], axis=1)
            merged = merged + rotated
        return merged.astype(jnp.bfloat16)

    return lax.map(one_pair, jnp.arange(pair_count).astype(jnp.int32))


def reference(echo, chirp, beam_one, shift_one, frac_one, base_one, beam_two, shift_two, frac_two, base_two):
    compressed = correlate_all(echo, chirp)
    level_one = merge_level(compressed, beam_one, shift_one, frac_one, base_one)
    level_two = merge_level(level_one, beam_two, shift_two, frac_two, base_two)
    grouped = level_two.reshape(N_PULSE // 4, N_REP, 2, 2, BD, 2, RANGE)
    return grouped.transpose(1, 0, 3, 2, 4, 5, 6).reshape(N_REP, N_PULSE, BD, 2, RANGE)
```

```python
import functools
import math

import jax
import jax.numpy as jnp
from jax import lax
from jax.experimental import pallas as pl
from jax.experimental.pallas import tpu as pltpu
from jax.sharding import PartitionSpec as P

LANES = 128
GROUP = 4
LEFT = 1
RIGHT = 5
MESH = pl.DeviceIdType.MESH


def block_of(member):
    return 2 * lax.rem(member, 2) + member // 2


def gather_kernel(chirp_ref, echo_ref, out_ref, ext, toeplitz, send_sem, recv_sem, local_sem):
    chunks = echo_ref.shape[1]
    taps = chirp_ref.shape[1]
    x = lax.axis_index("range")
    last = lax.axis_size("range") - 1
    z = lax.axis_index("pulse")
    first_member = z // GROUP * GROUP
    me = lax.rem(z, GROUP)
    has_left = x > 0
    has_right = x < last

    barrier = pltpu.get_barrier_semaphore()

    def greet(dx, dz):
        pl.semaphore_signal(
            barrier,
            inc=1,
            device_id={"range": x + dx, "pulse": first_member + lax.rem(me + dz, GROUP)},
            device_id_type=MESH,
        )

    for dz in range(1, GROUP):
        greet(0, dz)

    @pl.when(has_left)
    def _():
        for dz in range(GROUP):
            greet(-1, dz)

    @pl.when(has_right)
    def _():
        for dz in range(GROUP):
            greet(1, dz)

    def copy_to(kind, dz):
        member = lax.rem(me + dz, GROUP)
        block = block_of(member)
        dx = (0, -1, 1)[kind]
        start, count = ((0, chunks), (0, RIGHT), (chunks - LEFT, LEFT))[kind]
        target = (LEFT, LEFT + chunks, 0)[kind]
        return pltpu.make_async_remote_copy(
            src_ref=echo_ref.at[block, pl.ds(start, count)],
            dst_ref=ext.at[me, pl.ds(target, count)],
            send_sem=send_sem.at[kind, dz],
            recv_sem=recv_sem.at[kind, me],
            device_id={"range": x + dx, "pulse": first_member + member},
            device_id_type=MESH,
        )

    def arrival(kind, source):
        count = (chunks, RIGHT, LEFT)[kind]
        target = (LEFT, LEFT + chunks, 0)[kind]
        return pltpu.make_async_remote_copy(
            src_ref=ext.at[source, pl.ds(target, count)],
            dst_ref=ext.at[source, pl.ds(target, count)],
            send_sem=send_sem.at[kind, 0],
            recv_sem=recv_sem.at[kind, source],
            device_id={"range": x, "pulse": z},
            device_id_type=MESH,
        )

    own = pltpu.make_async_copy(
        echo_ref.at[block_of(me)], ext.at[me, pl.ds(LEFT, chunks)], local_sem
    )
    own.start()
    waits = GROUP - 1 + GROUP * (has_left.astype(jnp.int32) + has_right.astype(jnp.int32))
    pl.semaphore_wait(barrier, waits)

    for dz in (0, 2, 1, 3):

        @pl.when(has_left)
        def _():
            copy_to(1, dz).start()

        @pl.when(has_right)
        def _():
            copy_to(2, dz).start()

    for dz in (2, 1, 3):
        copy_to(0, dz).start()

    @pl.when(jnp.logical_not(has_right))
    def _():
        ext[:, LEFT + chunks :] = jnp.zeros((GROUP, RIGHT, 16, LANES), ext.dtype)

    @pl.when(jnp.logical_not(has_left))
    def _():
        ext[:, :LEFT] = jnp.zeros((GROUP, LEFT, 16, LANES), ext.dtype)

    span = 256 + taps
    for part in range(2):
        row = jnp.concatenate(
            [chirp_ref[part : part + 1, :].astype(jnp.float32), jnp.zeros((1, 256), jnp.float32)],
            axis=1,
        )
        rows = jnp.broadcast_to(row, (256, span))
        rolled = pltpu.roll(rows, 0, 1, stride=1, stride_axis=0)
        toeplitz[256 * part : 256 * (part + 1), :] = rolled.astype(toeplitz.dtype)

    out_blocks = (chunks + 2) // 2
    left_scale = has_left.astype(jnp.float32)
    right_scale = has_right.astype(jnp.float32)

    for dz in range(GROUP):
        source = lax.rem(me + dz, GROUP)
        if dz == 0:
            own.wait()
        else:
            arrival(0, source).wait_recv()

        @pl.when(has_right)
        def _():
            arrival(1, source).wait_recv()

        @pl.when(has_left)
        def _():
            arrival(2, source).wait_recv()

        held = ext[source].reshape((LEFT + chunks + RIGHT) // 2, 2, 16, LANES)
        pieces = [
            held[u // 2 : u // 2 + out_blocks, u % 2].reshape(out_blocks * 16, LANES)
            for u in range(span // LANES)
        ]
        windows = jnp.concatenate(pieces, axis=1)
        product = lax.dot_general(
            windows, toeplitz[...], (((1,), (1,)), ((), ())), preferred_element_type=jnp.float32
        )
        for block in range(out_blocks):
            up = product[16 * block : 16 * block + 8]
            down = product[16 * block + 8 : 16 * block + 16]
            values = (up[:, :256] + down[:, 256:], down[:, :256] - up[:, 256:])
            for half in range(2):
                chunk = 2 * block + half
                for part in range(2):
                    value = values[part][:, half * LANES : (half + 1) * LANES]
                    if chunk == 0:
                        value = value * left_scale
                    if chunk == chunks + 1:
                        value = value * right_scale
                    out_ref[source, pl.ds(32 * part + chunk, 8, stride=64), :] = value

    for dz in range(GROUP):

        @pl.when(has_left)
        def _():
            copy_to(1, dz).wait_send()

        @pl.when(has_right)
        def _():
            copy_to(2, dz).wait_send()

        if dz:
            copy_to(0, dz).wait_send()


def shifted(value, distance):
    rows = value.shape[0]
    turned = pltpu.roll(value, LANES - distance, 1)
    below = pltpu.roll(turned, rows - 1, 0)
    lane = lax.broadcasted_iota(jnp.int32, value.shape, 1)
    return jnp.where(lane < LANES - distance, turned, below)


def cos_sin(angle):
    turns = angle * (1.0 / (2.0 * math.pi))
    turns = turns - jnp.round(turns)
    half = turns * math.pi
    square = half * half
    sine = jnp.full_like(half, -1.0 / math.factorial(11))
    for n in (9, 7, 5, 3, 1):
        sine = sine * square + (-1.0) ** ((n - 1) // 2) / math.factorial(n)
    sine = sine * half
    cosine = jnp.full_like(half, 1.0 / math.factorial(12))
    for n in (10, 8, 6, 4, 2, 0):
        cosine = cosine * square + (-1.0) ** (n // 2) / math.factorial(n)
    return 1.0 - 2.0 * sine * sine, 2.0 * sine * cosine


def merge_kernel(
    beam_one, shift_one, frac_one, base_one, beam_two, shift_two, frac_two, base_two, taps,
    comp_ref, out_ref, zero_taps, one_taps,
):
    count_one = beam_one.shape[1]
    count_two = beam_two.shape[1]
    rows_out = out_ref.shape[1]
    bins = rows_out * LANES
    x = lax.axis_index("range")
    bin_total = bins * lax.axis_size("range")
    first_bin = x * bins
    z = lax.axis_index("pulse")
    block = 4 * lax.axis_index("rep") + block_of(lax.rem(z, GROUP))

    def spread(index, _):
        value = comp_ref[index]
        zero_taps[0, index] = value
        for t in range(1, 4):
            zero_taps[t, index] = shifted(value, t)
        return 0

    lax.fori_loop(0, comp_ref.shape[0], spread, 0)

    def positions(rows, margin):
        row = lax.broadcasted_iota(jnp.int32, (rows, LANES), 0)
        lane = lax.broadcasted_iota(jnp.int32, (rows, LANES), 1)
        return first_bin - margin + row * LANES + lane

    def factors(base, slope, rows, ramp):
        cosine, sine = cos_sin(base + slope * ramp)
        step = jnp.full((8, LANES), slope * (8.0 * LANES / bin_total), jnp.float32)
        step_cos, step_sin = cos_sin(step)
        cosines, sines = [cosine], [sine]
        for _ in range(rows // 8 - 1):
            cosine, sine = cosine * step_cos - sine * step_sin, sine * step_cos + cosine * step_sin
            cosines.append(cosine)
            sines.append(sine)
        return jnp.concatenate(cosines, 0), jnp.concatenate(sines, 0)

    def sampled(source, index, weights, distance, rows):
        early = weights[0] * source[0, index]
        late = weights[4] * source[0, index]
        for t in range(1, 4):
            value = source[t, index]
            early = early + weights[t] * value
            late = late + weights[t + 4] * value
        return shifted(early + shifted(late, 4), distance)[:rows]

    ramp_one = positions(8, 32).astype(jnp.float32) * (1.0 / bin_total) - 0.5
    place_one = positions(32, 32)
    inside_one = (place_one >= 0) & (place_one < bin_total)

    def first_merge(i, _):
        p = block * 16 + i
        sums = [[None, None], [None, None]]
        for c in range(2):
            beam = beam_one[c, p] - block * 8
            shift = shift_one[c, p]
            slope = 0.5 * (shift.astype(jnp.float32) + frac_one[c, p])
            cosine, sine = factors(base_one[c, p], slope, 32, ramp_one)
            weights = [taps[(c * (count_one + count_two) + p) * 8 + t] for t in range(8)]
            for q in range(2):
                index = ((2 * q + c) * 8 + beam) * 2
                real = sampled(zero_taps, index, weights, shift + 93, 32)
                imag = sampled(zero_taps, index + 1, weights, shift + 93, 32)
                turned = (real * cosine - imag * sine, real * sine + imag * cosine)
                for part in range(2):
                    if c == 0:
                        sums[q][part] = turned[part]
                    else:
                        sums[q][part] = sums[q][part] + turned[part]
        for q in range(2):
            for part in range(2):
                value = jnp.where(inside_one, sums[q][part], 0.0)
                index = (16 * q + i) * 2 + part
                one_taps[0, index] = value
                for t in range(1, 4):
                    one_taps[t, index] = shifted(value, t)
        return 0

    lax.fori_loop(0, 16, first_merge, 0)

    ramp_two = positions(8, 0).astype(jnp.float32) * (1.0 / bin_total) - 0.5

    def second_merge(i, _):
        p = block * 32 + i
        sums = [None, None]
        for c in range(2):
            beam = beam_two[c, p] - block * 16
            shift = shift_two[c, p]
            slope = 0.5 * (shift.astype(jnp.float32) + frac_two[c, p])
            cosine, sine = factors(base_two[c, p], slope, rows_out, ramp_two)
            weights = [
                taps[(c * (count_one + count_two) + count_one + p) * 8 + t] for t in range(8)
            ]
            index = (16 * c + beam) * 2
            real = sampled(one_taps, index, weights, shift + 29, rows_out)
            imag = sampled(one_taps, index + 1, weights, shift + 29, rows_out)
            turned = (real * cosine - imag * sine, real * sine + imag * cosine)
            for part in range(2):
                sums[part] = turned[part] if c == 0 else sums[part] + turned[part]
        for part in range(2):
            out_ref[2 * i + part] = sums[part].astype(out_ref.dtype)
        return 0

    lax.fori_loop(0, out_ref.shape[0] // 2, second_merge, 0)


def body(
    echo, chirp, beam_one, shift_one, frac_one, base_one, beam_two, shift_two, frac_two, base_two
):
    beams, _, bins = echo.shape[1:]
    chunks = bins // LANES
    taps = chirp.shape[1]
    arranged = echo[0].reshape(GROUP, 8, 2, chunks, LANES).transpose(0, 3, 2, 1, 4)
    arranged = arranged.reshape(GROUP, chunks, 16, LANES)
    vmem = pl.BlockSpec(memory_space=pltpu.VMEM)
    smem = pl.BlockSpec(memory_space=pltpu.SMEM)
    compressed = pl.pallas_call(
        gather_kernel,
        out_shape=jax.ShapeDtypeStruct((GROUP, 8 * 2 * 32, LANES), jnp.float32),
        in_specs=[vmem, pl.BlockSpec(memory_space=pl.ANY)],
        out_specs=vmem,
        scratch_shapes=[
            pltpu.VMEM((GROUP, LEFT + chunks + RIGHT, 16, LANES), jnp.bfloat16),
            pltpu.VMEM((512, 256 + taps), jnp.bfloat16),
            pltpu.SemaphoreType.DMA((3, GROUP)),
            pltpu.SemaphoreType.DMA((3, GROUP)),
            pltpu.SemaphoreType.DMA,
        ],
        compiler_params=pltpu.CompilerParams(
            collective_id=0, has_side_effects=True, vmem_limit_bytes=32 * 2**20
        ),
        name="gather_compress",
    )(chirp, arranged)

    fracs = jnp.concatenate([frac_one, frac_two], axis=1)
    spread = (jnp.arange(8).astype(jnp.float32) - 3.0)[None, None, :] - fracs[..., None]
    weights = jnp.sinc(spread) * (0.54 + 0.46 * jnp.cos(jnp.pi * spread / 4.0))
    merged = pl.pallas_call(
        merge_kernel,
        out_shape=jax.ShapeDtypeStruct((beams * 2, chunks, LANES), jnp.bfloat16),
        in_specs=[smem] * 9 + [vmem],
        out_specs=vmem,
        scratch_shapes=[
            pltpu.VMEM((4, GROUP * 8 * 2, 32, LANES), jnp.float32),
            pltpu.VMEM((4, 2 * 16 * 2, 32, LANES), jnp.float32),
        ],
        compiler_params=pltpu.CompilerParams(vmem_limit_bytes=32 * 2**20),
        name="merge",
    )(
        beam_one, shift_one, frac_one, base_one, beam_two, shift_two, frac_two, base_two,
        weights.reshape(-1), compressed.reshape(GROUP * 8 * 2, 32, LANES),
    )
    return merged.reshape(1, 1, beams, 2, bins)


def solution(mesh):
    in_specs = (
        P(("scene", "pulse"), "rep", None, "range"),
        P(),
        P(),
        P(),
        P(),
        P(),
        P(),
        P(),
        P(),
        P(),
    )
    out_specs = P("rep", ("scene", "pulse"), None, None, "range")
    return jax.shard_map(body, mesh=mesh, in_specs=in_specs, out_specs=out_specs, check_vma=False)
```

```python
import math

import jax
import jax.numpy as jnp
from jax import lax
from jax.experimental import pallas as pl
from jax.experimental.pallas import tpu as pltpu
from jax.sharding import PartitionSpec as P

LANES = 128
GROUP = 4
LEFT = 1
RIGHT = 5
ORDER = (1, 2, 3)
U_SPREAD, U_TURN, U_ONE, U_TWO = 8, 4, 4, 4
MESH = pl.DeviceIdType.MESH


def block_of(member):
    return 2 * lax.rem(member, 2) + member // 2


def shifted(value, distance):
    rows = value.shape[0]
    turned = pltpu.roll(value, LANES - distance, 1)
    below = pltpu.roll(turned, rows - 1, 0)
    lane = lax.broadcasted_iota(jnp.int32, value.shape, 1)
    return jnp.where(lane < LANES - distance, turned, below)


def cos_sin(angle):
    turns = angle * (1.0 / (2.0 * math.pi))
    turns = turns - jnp.round(turns)
    half = turns * math.pi
    square = half * half
    sine = jnp.full_like(half, -1.0 / math.factorial(11))
    for n in (9, 7, 5, 3, 1):
        sine = sine * square + (-1.0) ** ((n - 1) // 2) / math.factorial(n)
    sine = sine * half
    cosine = jnp.full_like(half, 1.0 / math.factorial(12))
    for n in (10, 8, 6, 4, 2, 0):
        cosine = cosine * square + (-1.0) ** (n // 2) / math.factorial(n)
    return 1.0 - 2.0 * sine * sine, 2.0 * sine * cosine


def partner(me, distance):
    member = me
    if distance % 2:
        member = member + 1 - 2 * lax.rem(me, 2)
    if distance // 2:
        member = member + 2 - 4 * (me // 2)
    return member


def kernel(
    chirp_ref, echo_ref, beam_one, shift_one, frac_one, base_one, beam_two, shift_two, frac_two,
    base_two, taps_ref, out_ref, ext, toeplitz, laid, zero_taps, one_taps, turn_one, turn_two, send_sem,
    recv_sem, local_sem,
):
    chunks = echo_ref.shape[1]
    taps = chirp_ref.shape[1]
    x = lax.axis_index("range")
    last = lax.axis_size("range") - 1
    z = lax.axis_index("pulse")
    first_member = z // GROUP * GROUP
    me = lax.rem(z, GROUP)
    has_left = x > 0
    has_right = x < last

    barrier = pltpu.get_barrier_semaphore()

    def greet(dx, dz):
        pl.semaphore_signal(
            barrier,
            inc=1,
            device_id={"range": x + dx, "pulse": first_member + partner(me, dz)},
            device_id_type=MESH,
        )

    for dz in range(1, GROUP):
        greet(0, dz)

    @pl.when(has_left)
    def _():
        for dz in range(GROUP):
            greet(-1, dz)

    @pl.when(has_right)
    def _():
        for dz in range(GROUP):
            greet(1, dz)

    def copy_to(kind, dz):
        member = partner(me, dz)
        block = block_of(member)
        dx = (0, -1, 1)[kind]
        start, count = ((0, chunks), (0, RIGHT), (chunks - LEFT, LEFT))[kind]
        target = (LEFT, LEFT + chunks, 0)[kind]
        return pltpu.make_async_remote_copy(
            src_ref=echo_ref.at[block, pl.ds(start, count)],
            dst_ref=ext.at[me, pl.ds(target, count)],
            send_sem=send_sem.at[kind, dz],
            recv_sem=recv_sem.at[kind, me],
            device_id={"range": x + dx, "pulse": first_member + member},
            device_id_type=MESH,
        )

    def arrival(kind, source):
        count = (chunks, RIGHT, LEFT)[kind]
        target = (LEFT, LEFT + chunks, 0)[kind]
        return pltpu.make_async_remote_copy(
            src_ref=ext.at[source, pl.ds(target, count)],
            dst_ref=ext.at[source, pl.ds(target, count)],
            send_sem=send_sem.at[kind, 0],
            recv_sem=recv_sem.at[kind, source],
            device_id={"range": x, "pulse": z},
            device_id_type=MESH,
        )

    own = pltpu.make_async_copy(
        echo_ref.at[block_of(me)], ext.at[me, pl.ds(LEFT, chunks)], local_sem
    )
    own.start()
    waits = GROUP - 1 + GROUP * (has_left.astype(jnp.int32) + has_right.astype(jnp.int32))
    pl.semaphore_wait(barrier, waits)

    def send_edges(dz):
        @pl.when(has_left)
        def _():
            copy_to(1, dz).start()

        @pl.when(has_right)
        def _():
            copy_to(2, dz).start()

    send_edges(0)
    for dz in ORDER:
        copy_to(0, dz).start()
        send_edges(dz)

    @pl.when(jnp.logical_not(has_right))
    def _():
        ext[:, LEFT + chunks :] = jnp.zeros((GROUP, RIGHT, 16, LANES), ext.dtype)

    @pl.when(jnp.logical_not(has_left))
    def _():
        ext[:, :LEFT] = jnp.zeros((GROUP, LEFT, 16, LANES), ext.dtype)

    span = 256 + taps
    for part in range(2):
        row = jnp.concatenate(
            [chirp_ref[part : part + 1, :].astype(jnp.float32), jnp.zeros((1, 256), jnp.float32)],
            axis=1,
        )
        rows = jnp.broadcast_to(row, (256, span))
        rolled = pltpu.roll(rows, 0, 1, stride=1, stride_axis=0)
        toeplitz[256 * part : 256 * (part + 1), :] = rolled.astype(toeplitz.dtype)

    out_blocks = (chunks + 2) // 2
    left_scale = has_left.astype(jnp.float32)
    right_scale = has_right.astype(jnp.float32)

    count_one = beam_one.shape[1]
    count_two = beam_two.shape[1]
    rows_out = out_ref.shape[1]
    bins = rows_out * LANES
    bin_total = bins * lax.axis_size("range")
    first_bin = x * bins
    block = 4 * lax.axis_index("rep") + block_of(me)

    def positions(rows, margin):
        row = lax.broadcasted_iota(jnp.int32, (rows, LANES), 0)
        lane = lax.broadcasted_iota(jnp.int32, (rows, LANES), 1)
        return first_bin - margin + row * LANES + lane

    def factors(base, slope, rows, ramp):
        cosine, sine = cos_sin(base + slope * ramp)
        step = jnp.full((8, LANES), slope * (8.0 * LANES / bin_total), jnp.float32)
        step_cos, step_sin = cos_sin(step)
        cosines, sines = [cosine], [sine]
        for _ in range(rows // 8 - 1):
            cosine, sine = cosine * step_cos - sine * step_sin, sine * step_cos + cosine * step_sin
            cosines.append(cosine)
            sines.append(sine)
        return jnp.concatenate(cosines, 0), jnp.concatenate(sines, 0)

    def sampled(load, weights, distance, rows):
        value = load(0)
        early = weights[0] * value
        late = weights[4] * value
        for t in range(1, 4):
            value = load(t)
            early = early + weights[t] * value
            late = late + weights[t + 4] * value
        return shifted(early + shifted(late, 4), distance)[:rows]

    ramp_one = positions(8, 32).astype(jnp.float32) * (1.0 / bin_total) - 0.5
    place_one = positions(32, 32)
    inside_one = (place_one >= 0) & (place_one < bin_total)

    ramp_two = positions(8, 0).astype(jnp.float32) * (1.0 / bin_total) - 0.5

    def turns(i, _):
        for c in range(2):
            p = block * 32 + i
            slope = 0.5 * (shift_two[c, p].astype(jnp.float32) + frac_two[c, p])
            cosine, sine = factors(base_two[c, p], slope, rows_out, ramp_two)
            turn_two[(2 * i + c) * 2] = cosine
            turn_two[(2 * i + c) * 2 + 1] = sine
        return 0

    def turns_one(i, _):
        for c in range(2):
            p = block * 16 + i
            slope = 0.5 * (shift_one[c, p].astype(jnp.float32) + frac_one[c, p])
            cosine, sine = factors(base_one[c, p], slope, 32, ramp_one)
            turn_one[(2 * i + c) * 2] = cosine
            turn_one[(2 * i + c) * 2 + 1] = sine
        return 0

    lax.fori_loop(0, 16, turns_one, 0, unroll=U_TURN)
    lax.fori_loop(0, 32, turns, 0, unroll=U_TURN)

    def compress(dz):
        source = partner(me, dz)
        if dz == 0:
            own.wait()
        else:
            arrival(0, source).wait_recv()

        @pl.when(has_right)
        def _():
            arrival(1, source).wait_recv()

        @pl.when(has_left)
        def _():
            arrival(2, source).wait_recv()

        held = ext[source].reshape((LEFT + chunks + RIGHT) // 2, 2, 16, LANES)
        pieces = [
            held[u // 2 : u // 2 + out_blocks, u % 2].reshape(out_blocks * 16, LANES)
            for u in range(span // LANES)
        ]
        windows = jnp.concatenate(pieces, axis=1)
        product = lax.dot_general(
            windows, toeplitz[...], (((1,), (1,)), ((), ())), preferred_element_type=jnp.float32
        )
        for block in range(out_blocks):
            up = product[16 * block : 16 * block + 8]
            down = product[16 * block + 8 : 16 * block + 16]
            values = (up[:, :256] + down[:, 256:], down[:, :256] - up[:, 256:])
            for half in range(2):
                chunk = 2 * block + half
                for part in range(2):
                    value = values[part][:, half * LANES : (half + 1) * LANES]
                    if chunk == 0:
                        value = value * left_scale
                    if chunk == chunks + 1:
                        value = value * right_scale
                    laid[pl.ds(32 * part + chunk, 8, stride=64), :] = value

        def spread(index, _):
            rows = pl.ds(pl.multiple_of(index * 32, 32), 32)
            value = laid[rows]
            zero_taps[0, source * 16 + index] = value
            for t in range(1, 4):
                zero_taps[t, source * 16 + index] = shifted(value, t)
            return 0

        lax.fori_loop(0, 16, spread, 0, unroll=U_SPREAD)

    def first_merges(q):
        def first_merge(i, _):
            p = block * 16 + i
            sums = [None, None]
            for c in range(2):
                beam = jnp.clip(beam_one[c, p] - block * 8, 0, 7)
                distance = shift_one[c, p] + 93
                weights = [taps_ref[(c * (count_one + count_two) + p) * 8 + t] for t in range(8)]
                parts = []
                for part in range(2):
                    index = (2 * q + c) * 16 + beam * 2 + part
                    parts.append(sampled(lambda t: zero_taps[t, index], weights, distance, 32))
                real, imag = parts
                cosine = turn_one[(2 * i + c) * 2]
                sine = turn_one[(2 * i + c) * 2 + 1]
                turned = (real * cosine - imag * sine, real * sine + imag * cosine)
                for part in range(2):
                    sums[part] = turned[part] if c == 0 else sums[part] + turned[part]
            for part in range(2):
                value = jnp.where(inside_one, sums[part], 0.0)
                index = (16 * q + i) * 2 + part
                one_taps[0, index] = value
                for t in range(1, 4):
                    one_taps[t, index] = shifted(value, t)
            return 0

        lax.fori_loop(0, 16, first_merge, 0, unroll=U_ONE)

    def second_merge(i, _):
        p = block * 32 + i
        sums = [None, None]
        for c in range(2):
            beam = jnp.clip(beam_two[c, p] - block * 16, 0, 15)
            distance = shift_two[c, p] + 29
            weights = [
                taps_ref[(c * (count_one + count_two) + count_one + p) * 8 + t] for t in range(8)
            ]
            parts = []
            for part in range(2):
                index = (16 * c + beam) * 2 + part
                parts.append(sampled(lambda t: one_taps[t, index], weights, distance, rows_out))
            real, imag = parts
            cosine = turn_two[(2 * i + c) * 2]
            sine = turn_two[(2 * i + c) * 2 + 1]
            turned = (real * cosine - imag * sine, real * sine + imag * cosine)
            for part in range(2):
                sums[part] = turned[part] if c == 0 else sums[part] + turned[part]
        for part in range(2):
            out_ref[2 * i + part] = sums[part].astype(out_ref.dtype)
        return 0

    compress(0)
    compress(1)
    first_merges(me // 2)
    compress(2)
    compress(3)
    first_merges(1 - me // 2)
    lax.fori_loop(0, 32, second_merge, 0, unroll=U_TWO)

    for dz in range(GROUP):

        @pl.when(has_left)
        def _():
            copy_to(1, dz).wait_send()

        @pl.when(has_right)
        def _():
            copy_to(2, dz).wait_send()

        if dz:
            copy_to(0, dz).wait_send()


def body(
    echo, chirp, beam_one, shift_one, frac_one, base_one, beam_two, shift_two, frac_two, base_two
):
    beams, _, bins = echo.shape[1:]
    chunks = bins // LANES
    taps = chirp.shape[1]
    arranged = echo[0].reshape(GROUP, 8, 2, chunks, LANES).transpose(0, 3, 2, 1, 4)
    arranged = arranged.reshape(GROUP, chunks, 16, LANES)
    vmem = pl.BlockSpec(memory_space=pltpu.VMEM)
    smem = pl.BlockSpec(memory_space=pltpu.SMEM)
    fracs = jnp.concatenate([frac_one, frac_two], axis=1)
    spread = (jnp.arange(8).astype(jnp.float32) - 3.0)[None, None, :] - fracs[..., None]
    weights = jnp.sinc(spread) * (0.54 + 0.46 * jnp.cos(jnp.pi * spread / 4.0))
    merged = pl.pallas_call(
        kernel,
        out_shape=jax.ShapeDtypeStruct((beams * 2, chunks, LANES), jnp.bfloat16),
        in_specs=[vmem, pl.BlockSpec(memory_space=pl.ANY)] + [smem] * 9,
        out_specs=vmem,
        scratch_shapes=[
            pltpu.VMEM((GROUP, LEFT + chunks + RIGHT, 16, LANES), jnp.bfloat16),
            pltpu.VMEM((512, 256 + taps), jnp.bfloat16),
            pltpu.VMEM((8 * 2 * 32, LANES), jnp.float32),
            pltpu.VMEM((4, GROUP * 16, 32, LANES), jnp.float32),
            pltpu.VMEM((4, 2 * 16 * 2, 32, LANES), jnp.float32),
            pltpu.VMEM((16 * 2 * 2, 32, LANES), jnp.float32),
            pltpu.VMEM((32 * 2 * 2, chunks, LANES), jnp.float32),
            pltpu.SemaphoreType.DMA((3, GROUP)),
            pltpu.SemaphoreType.DMA((3, GROUP)),
            pltpu.SemaphoreType.DMA,
        ],
        compiler_params=pltpu.CompilerParams(
            collective_id=0, has_side_effects=True, vmem_limit_bytes=40 * 2**20
        ),
        name="merge_all",
    )(
        chirp, arranged, beam_one, shift_one, frac_one, base_one, beam_two, shift_two, frac_two,
        base_two, weights.reshape(-1),
    )
    return merged.reshape(1, 1, beams, 2, bins)


def solution(mesh):
    in_specs = (
        P(("scene", "pulse"), "rep", None, "range"),
        P(),
        P(),
        P(),
        P(),
        P(),
        P(),
        P(),
        P(),
        P(),
    )
    out_specs = P("rep", ("scene", "pulse"), None, None, "range")
    return jax.shard_map(body, mesh=mesh, in_specs=in_specs, out_specs=out_specs, check_vma=False)
```

```python
import math

import jax
import jax.numpy as jnp
from jax import lax
from jax.experimental import pallas as pl
from jax.experimental.pallas import tpu as pltpu
from jax.sharding import PartitionSpec as P

LANES = 128
GROUP = 4
LEFT = 1
RIGHT = 5
ORDER = (1, 2, 3)
U_SPREAD, U_TURN, U_ONE, U_TWO = 8, 4, 4, 4
MESH = pl.DeviceIdType.MESH


def block_of(member):
    return 2 * lax.rem(member, 2) + member // 2


def shifted(value, distance):
    rows = value.shape[0]
    turned = pltpu.roll(value, LANES - distance, 1)
    below = pltpu.roll(turned, rows - 1, 0)
    lane = lax.broadcasted_iota(jnp.int32, value.shape, 1)
    return jnp.where(lane < LANES - distance, turned, below)


def cos_sin(angle):
    turns = angle * (1.0 / (2.0 * math.pi))
    turns = turns - jnp.round(turns)
    half = turns * math.pi
    square = half * half
    sine = jnp.full_like(half, -1.0 / math.factorial(11))
    for n in (9, 7, 5, 3, 1):
        sine = sine * square + (-1.0) ** ((n - 1) // 2) / math.factorial(n)
    sine = sine * half
    cosine = jnp.full_like(half, 1.0 / math.factorial(12))
    for n in (10, 8, 6, 4, 2, 0):
        cosine = cosine * square + (-1.0) ** (n // 2) / math.factorial(n)
    return 1.0 - 2.0 * sine * sine, 2.0 * sine * cosine


def tap_weights(frac):
    tap = lax.broadcasted_iota(jnp.int32, frac.shape, 0)
    spread = (tap.astype(jnp.float32) - 3.0) - frac
    near = jnp.minimum(frac, 1.0 - frac) * math.pi
    square = near * near
    sine = jnp.full_like(near, -1.0 / math.factorial(11))
    for n in (9, 7, 5, 3, 1):
        sine = sine * square + (-1.0) ** ((n - 1) // 2) / math.factorial(n)
    sine = jnp.where(lax.rem(tap, 2) == 0, sine, -sine) * near
    exact = spread == 0.0
    sinc = jnp.where(exact, 1.0, sine / jnp.where(exact, 1.0, math.pi * spread))
    return sinc * (0.54 + 0.46 * cos_sin(spread * (math.pi / 4.0))[0])


def partner(me, distance):
    member = me
    if distance % 2:
        member = member + 1 - 2 * lax.rem(me, 2)
    if distance // 2:
        member = member + 2 - 4 * (me // 2)
    return member


def kernel(
    chirp_ref, echo_ref, beam_one, shift_one, frac_one, base_one, beam_two, shift_two, frac_two,
    base_two, fracs_one, fracs_two, out_ref, ext, taps_held, taps_ref, toeplitz, laid, zero_taps, one_taps, turn_one, turn_two, send_sem,
    recv_sem, local_sem, taps_sem,
):
    chunks = echo_ref.shape[1]
    taps = chirp_ref.shape[1]
    x = lax.axis_index("range")
    last = lax.axis_size("range") - 1
    z = lax.axis_index("pulse")
    first_member = z // GROUP * GROUP
    me = lax.rem(z, GROUP)
    has_left = x > 0
    has_right = x < last

    barrier = pltpu.get_barrier_semaphore()

    def greet(dx, dz):
        pl.semaphore_signal(
            barrier,
            inc=1,
            device_id={"range": x + dx, "pulse": first_member + partner(me, dz)},
            device_id_type=MESH,
        )

    for dz in range(1, GROUP):
        greet(0, dz)

    @pl.when(has_left)
    def _():
        for dz in range(GROUP):
            greet(-1, dz)

    @pl.when(has_right)
    def _():
        for dz in range(GROUP):
            greet(1, dz)

    def copy_to(kind, dz):
        member = partner(me, dz)
        block = block_of(member)
        dx = (0, -1, 1)[kind]
        start, count = ((0, chunks), (0, RIGHT), (chunks - LEFT, LEFT))[kind]
        target = (LEFT, LEFT + chunks, 0)[kind]
        return pltpu.make_async_remote_copy(
            src_ref=echo_ref.at[block, pl.ds(start, count)],
            dst_ref=ext.at[me, pl.ds(target, count)],
            send_sem=send_sem.at[kind, dz],
            recv_sem=recv_sem.at[kind, me],
            device_id={"range": x + dx, "pulse": first_member + member},
            device_id_type=MESH,
        )

    def arrival(kind, source):
        count = (chunks, RIGHT, LEFT)[kind]
        target = (LEFT, LEFT + chunks, 0)[kind]
        return pltpu.make_async_remote_copy(
            src_ref=ext.at[source, pl.ds(target, count)],
            dst_ref=ext.at[source, pl.ds(target, count)],
            send_sem=send_sem.at[kind, 0],
            recv_sem=recv_sem.at[kind, source],
            device_id={"range": x, "pulse": z},
            device_id_type=MESH,
        )

    own = pltpu.make_async_copy(
        echo_ref.at[block_of(me)], ext.at[me, pl.ds(LEFT, chunks)], local_sem
    )
    own.start()
    waits = GROUP - 1 + GROUP * (has_left.astype(jnp.int32) + has_right.astype(jnp.int32))
    pl.semaphore_wait(barrier, waits)

    def send_edges(dz):
        @pl.when(has_left)
        def _():
            copy_to(1, dz).start()

        @pl.when(has_right)
        def _():
            copy_to(2, dz).start()

    send_edges(0)
    for dz in ORDER:
        copy_to(0, dz).start()
        send_edges(dz)

    @pl.when(jnp.logical_not(has_right))
    def _():
        ext[:, LEFT + chunks :] = jnp.zeros((GROUP, RIGHT, 16, LANES), ext.dtype)

    @pl.when(jnp.logical_not(has_left))
    def _():
        ext[:, :LEFT] = jnp.zeros((GROUP, LEFT, 16, LANES), ext.dtype)

    span = 256 + taps
    for part in range(2):
        row = jnp.concatenate(
            [chirp_ref[part : part + 1, :].astype(jnp.float32), jnp.zeros((1, 256), jnp.float32)],
            axis=1,
        )
        rows = jnp.broadcast_to(row, (256, span))
        rolled = pltpu.roll(rows, 0, 1, stride=1, stride_axis=0)
        toeplitz[256 * part : 256 * (part + 1), :] = rolled.astype(toeplitz.dtype)

    out_blocks = (chunks + 2) // 2
    left_scale = has_left.astype(jnp.float32)
    right_scale = has_right.astype(jnp.float32)

    count_one = beam_one.shape[1]
    rows_out = out_ref.shape[1]
    bins = rows_out * LANES
    bin_total = bins * lax.axis_size("range")
    first_bin = x * bins
    block = 4 * lax.axis_index("rep") + block_of(me)

    for c in range(2):
        frac = jnp.concatenate([fracs_one[c : c + 1, :], fracs_two[c : c + 1, :]], axis=1)
        frac = jnp.broadcast_to(frac, (8, frac.shape[1]))
        taps_held[8 * c : 8 * (c + 1), :] = tap_weights(frac)
    taps_copy = pltpu.make_async_copy(taps_held, taps_ref, taps_sem)
    taps_copy.start()

    def positions(rows, margin):
        row = lax.broadcasted_iota(jnp.int32, (rows, LANES), 0)
        lane = lax.broadcasted_iota(jnp.int32, (rows, LANES), 1)
        return first_bin - margin + row * LANES + lane

    def factors(base, slope, rows, ramp):
        cosine, sine = cos_sin(base + slope * ramp)
        step = jnp.full((8, LANES), slope * (8.0 * LANES / bin_total), jnp.float32)
        step_cos, step_sin = cos_sin(step)
        cosines, sines = [cosine], [sine]
        for _ in range(rows // 8 - 1):
            cosine, sine = cosine * step_cos - sine * step_sin, sine * step_cos + cosine * step_sin
            cosines.append(cosine)
            sines.append(sine)
        return jnp.concatenate(cosines, 0), jnp.concatenate(sines, 0)

    def sampled(load, weights, distance, rows):
        value = load(0)
        early = weights[0] * value
        late = weights[4] * value
        for t in range(1, 4):
            value = load(t)
            early = early + weights[t] * value
            late = late + weights[t + 4] * value
        return shifted(early + shifted(late, 4), distance)[:rows]

    ramp_one = positions(8, 32).astype(jnp.float32) * (1.0 / bin_total) - 0.5
    place_one = positions(32, 32)
    inside_one = (place_one >= 0) & (place_one < bin_total)

    ramp_two = positions(8, 0).astype(jnp.float32) * (1.0 / bin_total) - 0.5

    def turns(i, _):
        for c in range(2):
            p = block * 32 + i
            slope = 0.5 * (shift_two[c, p].astype(jnp.float32) + frac_two[c, p])
            cosine, sine = factors(base_two[c, p], slope, rows_out, ramp_two)
            turn_two[(2 * i + c) * 2] = cosine
            turn_two[(2 * i + c) * 2 + 1] = sine
        return 0

    def turns_one(i, _):
        for c in range(2):
            p = block * 16 + i
            slope = 0.5 * (shift_one[c, p].astype(jnp.float32) + frac_one[c, p])
            cosine, sine = factors(base_one[c, p], slope, 32, ramp_one)
            turn_one[(2 * i + c) * 2] = cosine
            turn_one[(2 * i + c) * 2 + 1] = sine
        return 0

    lax.fori_loop(0, 16, turns_one, 0, unroll=U_TURN)
    lax.fori_loop(0, 32, turns, 0, unroll=U_TURN)

    def compress(dz):
        source = partner(me, dz)
        if dz == 0:
            own.wait()
        else:
            arrival(0, source).wait_recv()

        @pl.when(has_right)
        def _():
            arrival(1, source).wait_recv()

        @pl.when(has_left)
        def _():
            arrival(2, source).wait_recv()

        held = ext[source].reshape((LEFT + chunks + RIGHT) // 2, 2, 16, LANES)
        pieces = [
            held[u // 2 : u // 2 + out_blocks, u % 2].reshape(out_blocks * 16, LANES)
            for u in range(span // LANES)
        ]
        windows = jnp.concatenate(pieces, axis=1)
        product = lax.dot_general(
            windows, toeplitz[...], (((1,), (1,)), ((), ())), preferred_element_type=jnp.float32
        )
        for block in range(out_blocks):
            up = product[16 * block : 16 * block + 8]
            down = product[16 * block + 8 : 16 * block + 16]
            values = (up[:, :256] + down[:, 256:], down[:, :256] - up[:, 256:])
            for half in range(2):
                chunk = 2 * block + half
                for part in range(2):
                    value = values[part][:, half * LANES : (half + 1) * LANES]
                    if chunk == 0:
                        value = value * left_scale
                    if chunk == chunks + 1:
                        value = value * right_scale
                    laid[pl.ds(32 * part + chunk, 8, stride=64), :] = value

        def spread(index, _):
            rows = pl.ds(pl.multiple_of(index * 32, 32), 32)
            value = laid[rows]
            zero_taps[0, source * 16 + index] = value
            for t in range(1, 4):
                zero_taps[t, source * 16 + index] = shifted(value, t)
            return 0

        lax.fori_loop(0, 16, spread, 0, unroll=U_SPREAD)

    def first_merges(q):
        def first_merge(i, _):
            p = block * 16 + i
            sums = [None, None]
            for c in range(2):
                beam = jnp.clip(beam_one[c, p] - block * 8, 0, 7)
                distance = shift_one[c, p] + 93
                weights = [taps_ref[8 * c + t, p] for t in range(8)]
                parts = []
                for part in range(2):
                    index = (2 * q + c) * 16 + beam * 2 + part
                    parts.append(sampled(lambda t: zero_taps[t, index], weights, distance, 32))
                real, imag = parts
                cosine = turn_one[(2 * i + c) * 2]
                sine = turn_one[(2 * i + c) * 2 + 1]
                turned = (real * cosine - imag * sine, real * sine + imag * cosine)
                for part in range(2):
                    sums[part] = turned[part] if c == 0 else sums[part] + turned[part]
            for part in range(2):
                value = jnp.where(inside_one, sums[part], 0.0)
                index = (16 * q + i) * 2 + part
                one_taps[0, index] = value
                for t in range(1, 4):
                    one_taps[t, index] = shifted(value, t)
            return 0

        lax.fori_loop(0, 16, first_merge, 0, unroll=U_ONE)

    def second_merge(i, _):
        p = block * 32 + i
        sums = [None, None]
        for c in range(2):
            beam = jnp.clip(beam_two[c, p] - block * 16, 0, 15)
            distance = shift_two[c, p] + 29
            weights = [
                taps_ref[8 * c + t, count_one + p] for t in range(8)
            ]
            parts = []
            for part in range(2):
                index = (16 * c + beam) * 2 + part
                parts.append(sampled(lambda t: one_taps[t, index], weights, distance, rows_out))
            real, imag = parts
            cosine = turn_two[(2 * i + c) * 2]
            sine = turn_two[(2 * i + c) * 2 + 1]
            turned = (real * cosine - imag * sine, real * sine + imag * cosine)
            for part in range(2):
                sums[part] = turned[part] if c == 0 else sums[part] + turned[part]
        for part in range(2):
            out_ref[2 * i + part] = sums[part].astype(out_ref.dtype)
        return 0

    taps_copy.wait()
    compress(0)
    compress(1)
    first_merges(me // 2)
    compress(2)
    compress(3)
    first_merges(1 - me // 2)
    lax.fori_loop(0, 32, second_merge, 0, unroll=U_TWO)

    for dz in range(GROUP):

        @pl.when(has_left)
        def _():
            copy_to(1, dz).wait_send()

        @pl.when(has_right)
        def _():
            copy_to(2, dz).wait_send()

        if dz:
            copy_to(0, dz).wait_send()


def body(
    echo, chirp, beam_one, shift_one, frac_one, base_one, beam_two, shift_two, frac_two, base_two
):
    beams, _, bins = echo.shape[1:]
    chunks = bins // LANES
    taps = chirp.shape[1]
    fracs = frac_one.shape[1] + frac_two.shape[1]
    arranged = echo[0].reshape(GROUP, 8, 2, chunks, LANES).transpose(0, 3, 2, 1, 4)
    arranged = arranged.reshape(GROUP, chunks, 16, LANES)
    vmem = pl.BlockSpec(memory_space=pltpu.VMEM)
    smem = pl.BlockSpec(memory_space=pltpu.SMEM)
    merged = pl.pallas_call(
        kernel,
        out_shape=jax.ShapeDtypeStruct((beams * 2, chunks, LANES), jnp.bfloat16),
        in_specs=[vmem, pl.BlockSpec(memory_space=pl.ANY)] + [smem] * 8 + [vmem] * 2,
        out_specs=vmem,
        scratch_shapes=[
            pltpu.VMEM((GROUP, LEFT + chunks + RIGHT, 16, LANES), jnp.bfloat16),
            pltpu.VMEM((16, fracs), jnp.float32),
            pltpu.SMEM((16, fracs), jnp.float32),
            pltpu.VMEM((512, 256 + taps), jnp.bfloat16),
            pltpu.VMEM((8 * 2 * 32, LANES), jnp.float32),
            pltpu.VMEM((4, GROUP * 16, 32, LANES), jnp.float32),
            pltpu.VMEM((4, 2 * 16 * 2, 32, LANES), jnp.float32),
            pltpu.VMEM((16 * 2 * 2, 32, LANES), jnp.float32),
            pltpu.VMEM((32 * 2 * 2, chunks, LANES), jnp.float32),
            pltpu.SemaphoreType.DMA((3, GROUP)),
            pltpu.SemaphoreType.DMA((3, GROUP)),
            pltpu.SemaphoreType.DMA,
            pltpu.SemaphoreType.DMA,
        ],
        compiler_params=pltpu.CompilerParams(
            collective_id=0, has_side_effects=True, vmem_limit_bytes=40 * 2**20
        ),
        name="merge_all",
    )(
        chirp, arranged, beam_one, shift_one, frac_one, base_one, beam_two, shift_two, frac_two,
        base_two, frac_one, frac_two,
    )
    return merged.reshape(1, 1, beams, 2, bins)


def solution(mesh):
    in_specs = (
        P(("scene", "pulse"), "rep", None, "range"),
        P(),
        P(),
        P(),
        P(),
        P(),
        P(),
        P(),
        P(),
        P(),
    )
    out_specs = P("rep", ("scene", "pulse"), None, None, "range")
    return jax.shard_map(body, mesh=mesh, in_specs=in_specs, out_specs=out_specs, check_vma=False)
```

```python
import math

import jax
import jax.numpy as jnp
from jax import lax
from jax.experimental import pallas as pl
from jax.experimental.pallas import tpu as pltpu
from jax.sharding import PartitionSpec as P

LANES = 128
GROUP = 4
LEFT = 1
RIGHT = 5
ORDER = (1, 2, 3)
U_SPREAD, U_TURN, U_ONE, U_TWO = 16, 4, 4, 4
MESH = pl.DeviceIdType.MESH


def block_of(member):
    return 2 * lax.rem(member, 2) + member // 2


def shifted(value, distance):
    rows = value.shape[0]
    turned = pltpu.roll(value, LANES - distance, 1)
    below = pltpu.roll(turned, rows - 1, 0)
    lane = lax.broadcasted_iota(jnp.int32, value.shape, 1)
    return jnp.where(lane < LANES - distance, turned, below)


def cos_sin(angle):
    turns = angle * (1.0 / (2.0 * math.pi))
    turns = turns - jnp.round(turns)
    half = turns * math.pi
    square = half * half
    sine = jnp.full_like(half, -1.0 / math.factorial(11))
    for n in (9, 7, 5, 3, 1):
        sine = sine * square + (-1.0) ** ((n - 1) // 2) / math.factorial(n)
    sine = sine * half
    cosine = jnp.full_like(half, 1.0 / math.factorial(12))
    for n in (10, 8, 6, 4, 2, 0):
        cosine = cosine * square + (-1.0) ** (n // 2) / math.factorial(n)
    return 1.0 - 2.0 * sine * sine, 2.0 * sine * cosine


def tap_weights(frac):
    tap = lax.broadcasted_iota(jnp.int32, frac.shape, 0)
    spread = (tap.astype(jnp.float32) - 3.0) - frac
    near = jnp.minimum(frac, 1.0 - frac) * math.pi
    square = near * near
    sine = jnp.full_like(near, -1.0 / math.factorial(11))
    for n in (9, 7, 5, 3, 1):
        sine = sine * square + (-1.0) ** ((n - 1) // 2) / math.factorial(n)
    sine = jnp.where(lax.rem(tap, 2) == 0, sine, -sine) * near
    exact = spread == 0.0
    sinc = jnp.where(exact, 1.0, sine / jnp.where(exact, 1.0, math.pi * spread))
    return sinc * (0.54 + 0.46 * cos_sin(spread * (math.pi / 4.0))[0])


def partner(me, distance):
    member = me
    if distance % 2:
        member = member + 1 - 2 * lax.rem(me, 2)
    if distance // 2:
        member = member + 2 - 4 * (me // 2)
    return member


def kernel(
    chirp_ref, echo_ref, beam_one, shift_one, frac_one, base_one, beam_two, shift_two, frac_two,
    base_two, fracs_one, fracs_two, out_ref, ext, taps_held, taps_ref, toeplitz, laid, zero_taps, one_taps, turn_one, turn_two, send_sem,
    recv_sem, local_sem, taps_sem,
):
    chunks = echo_ref.shape[1]
    taps = chirp_ref.shape[1]
    x = lax.axis_index("range")
    last = lax.axis_size("range") - 1
    z = lax.axis_index("pulse")
    first_member = z // GROUP * GROUP
    me = lax.rem(z, GROUP)
    has_left = x > 0
    has_right = x < last

    barrier = pltpu.get_barrier_semaphore()

    def greet(dx, dz):
        pl.semaphore_signal(
            barrier,
            inc=1,
            device_id={"range": x + dx, "pulse": first_member + partner(me, dz)},
            device_id_type=MESH,
        )

    for dz in range(1, GROUP):
        greet(0, dz)

    @pl.when(has_left)
    def _():
        for dz in range(GROUP):
            greet(-1, dz)

    @pl.when(has_right)
    def _():
        for dz in range(GROUP):
            greet(1, dz)

    def copy_to(kind, dz):
        member = partner(me, dz)
        block = block_of(member)
        dx = (0, -1, 1)[kind]
        start, count = ((0, chunks), (0, RIGHT), (chunks - LEFT, LEFT))[kind]
        target = (LEFT, LEFT + chunks, 0)[kind]
        return pltpu.make_async_remote_copy(
            src_ref=echo_ref.at[block, pl.ds(start, count)],
            dst_ref=ext.at[me, pl.ds(target, count)],
            send_sem=send_sem.at[kind, dz],
            recv_sem=recv_sem.at[kind, me],
            device_id={"range": x + dx, "pulse": first_member + member},
            device_id_type=MESH,
        )

    def arrival(kind, source):
        count = (chunks, RIGHT, LEFT)[kind]
        target = (LEFT, LEFT + chunks, 0)[kind]
        return pltpu.make_async_remote_copy(
            src_ref=ext.at[source, pl.ds(target, count)],
            dst_ref=ext.at[source, pl.ds(target, count)],
            send_sem=send_sem.at[kind, 0],
            recv_sem=recv_sem.at[kind, source],
            device_id={"range": x, "pulse": z},
            device_id_type=MESH,
        )

    own = pltpu.make_async_copy(
        echo_ref.at[block_of(me)], ext.at[me, pl.ds(LEFT, chunks)], local_sem
    )
    own.start()
    waits = GROUP - 1 + GROUP * (has_left.astype(jnp.int32) + has_right.astype(jnp.int32))
    pl.semaphore_wait(barrier, waits)

    def send_edges(dz):
        @pl.when(has_left)
        def _():
            copy_to(1, dz).start()

        @pl.when(has_right)
        def _():
            copy_to(2, dz).start()

    send_edges(0)
    for dz in ORDER:
        copy_to(0, dz).start()
        send_edges(dz)

    @pl.when(jnp.logical_not(has_right))
    def _():
        ext[:, LEFT + chunks :] = jnp.zeros((GROUP, RIGHT, 16, LANES), ext.dtype)

    @pl.when(jnp.logical_not(has_left))
    def _():
        ext[:, :LEFT] = jnp.zeros((GROUP, LEFT, 16, LANES), ext.dtype)

    span = 256 + taps
    for part in range(2):
        row = jnp.concatenate(
            [chirp_ref[part : part + 1, :].astype(jnp.float32), jnp.zeros((1, 256), jnp.float32)],
            axis=1,
        )
        rows = jnp.broadcast_to(row, (256, span))
        rolled = pltpu.roll(rows, 0, 1, stride=1, stride_axis=0)
        toeplitz[256 * part : 256 * (part + 1), :] = rolled.astype(toeplitz.dtype)

    out_blocks = (chunks + 2) // 2
    left_scale = has_left.astype(jnp.float32)
    right_scale = has_right.astype(jnp.float32)

    count_one = beam_one.shape[1]
    rows_out = out_ref.shape[1]
    bins = rows_out * LANES
    bin_total = bins * lax.axis_size("range")
    first_bin = x * bins
    block = 4 * lax.axis_index("rep") + block_of(me)

    for c in range(2):
        frac = jnp.concatenate([fracs_one[c : c + 1, :], fracs_two[c : c + 1, :]], axis=1)
        frac = jnp.broadcast_to(frac, (8, frac.shape[1]))
        taps_held[8 * c : 8 * (c + 1), :] = tap_weights(frac)
    taps_copy = pltpu.make_async_copy(taps_held, taps_ref, taps_sem)
    taps_copy.start()

    def positions(rows, margin):
        row = lax.broadcasted_iota(jnp.int32, (rows, LANES), 0)
        lane = lax.broadcasted_iota(jnp.int32, (rows, LANES), 1)
        return first_bin - margin + row * LANES + lane

    def factors(base, slope, rows, ramp):
        cosine, sine = cos_sin(base + slope * ramp)
        step = jnp.full((8, LANES), slope * (8.0 * LANES / bin_total), jnp.float32)
        step_cos, step_sin = cos_sin(step)
        cosines, sines = [cosine], [sine]
        for _ in range(rows // 8 - 1):
            cosine, sine = cosine * step_cos - sine * step_sin, sine * step_cos + cosine * step_sin
            cosines.append(cosine)
            sines.append(sine)
        return jnp.concatenate(cosines, 0), jnp.concatenate(sines, 0)

    def sampled(load, weights, distance, rows):
        value = load(0)
        early = weights[0] * value
        late = weights[4] * value
        for t in range(1, 4):
            value = load(t)
            early = early + weights[t] * value
            late = late + weights[t + 4] * value
        return shifted(early + shifted(late, 4), distance)[:rows]

    ramp_one = positions(8, 32).astype(jnp.float32) * (1.0 / bin_total) - 0.5
    place_one = positions(32, 32)
    inside_one = (place_one >= 0) & (place_one < bin_total)

    ramp_two = positions(8, 0).astype(jnp.float32) * (1.0 / bin_total) - 0.5

    def turns(i, _):
        for c in range(2):
            p = block * 32 + i
            slope = 0.5 * (shift_two[c, p].astype(jnp.float32) + frac_two[c, p])
            cosine, sine = factors(base_two[c, p], slope, rows_out, ramp_two)
            turn_two[(2 * i + c) * 2] = cosine
            turn_two[(2 * i + c) * 2 + 1] = sine
        return 0

    def turns_one(i, _):
        for c in range(2):
            p = block * 16 + i
            slope = 0.5 * (shift_one[c, p].astype(jnp.float32) + frac_one[c, p])
            cosine, sine = factors(base_one[c, p], slope, 32, ramp_one)
            turn_one[(2 * i + c) * 2] = cosine
            turn_one[(2 * i + c) * 2 + 1] = sine
        return 0

    lax.fori_loop(0, 16, turns_one, 0, unroll=U_TURN)
    lax.fori_loop(0, 32, turns, 0, unroll=U_TURN)

    def compress(dz):
        source = partner(me, dz)
        if dz == 0:
            own.wait()
        else:
            arrival(0, source).wait_recv()

        @pl.when(has_right)
        def _():
            arrival(1, source).wait_recv()

        @pl.when(has_left)
        def _():
            arrival(2, source).wait_recv()

        held = ext[source].reshape((LEFT + chunks + RIGHT) // 2, 2, 16, LANES)
        pieces = [
            held[u // 2 : u // 2 + out_blocks, u % 2].reshape(out_blocks * 16, LANES)
            for u in range(span // LANES)
        ]
        windows = jnp.concatenate(pieces, axis=1)
        product = lax.dot_general(
            windows, toeplitz[...], (((1,), (1,)), ((), ())), preferred_element_type=jnp.float32
        )
        for block in range(out_blocks):
            up = product[16 * block : 16 * block + 8]
            down = product[16 * block + 8 : 16 * block + 16]
            values = (up[:, :256] + down[:, 256:], down[:, :256] - up[:, 256:])
            for half in range(2):
                chunk = 2 * block + half
                for part in range(2):
                    value = values[part][:, half * LANES : (half + 1) * LANES]
                    if chunk == 0:
                        value = value * left_scale
                    if chunk == chunks + 1:
                        value = value * right_scale
                    laid[pl.ds(32 * part + chunk, 8, stride=64), :] = value

        def spread(index, _):
            rows = pl.ds(pl.multiple_of(index * 32, 32), 32)
            value = laid[rows]
            zero_taps[0, source * 16 + index] = value
            for t in range(1, 4):
                zero_taps[t, source * 16 + index] = shifted(value, t)
            return 0

        lax.fori_loop(0, 16, spread, 0, unroll=U_SPREAD)

    def first_merges(q):
        def first_merge(i, _):
            p = block * 16 + i
            sums = [None, None]
            for c in range(2):
                beam = jnp.clip(beam_one[c, p] - block * 8, 0, 7)
                distance = shift_one[c, p] + 93
                weights = [taps_ref[8 * c + t, p] for t in range(8)]
                parts = []
                for part in range(2):
                    index = (2 * q + c) * 16 + beam * 2 + part
                    parts.append(sampled(lambda t: zero_taps[t, index], weights, distance, 32))
                real, imag = parts
                cosine = turn_one[(2 * i + c) * 2]
                sine = turn_one[(2 * i + c) * 2 + 1]
                turned = (real * cosine - imag * sine, real * sine + imag * cosine)
                for part in range(2):
                    sums[part] = turned[part] if c == 0 else sums[part] + turned[part]
            for part in range(2):
                value = jnp.where(inside_one, sums[part], 0.0)
                index = (16 * q + i) * 2 + part
                one_taps[0, index] = value
                for t in range(1, 4):
                    one_taps[t, index] = shifted(value, t)
            return 0

        lax.fori_loop(0, 16, first_merge, 0, unroll=U_ONE)

    def second_merge(i, _):
        p = block * 32 + i
        sums = [None, None]
        for c in range(2):
            beam = jnp.clip(beam_two[c, p] - block * 16, 0, 15)
            distance = shift_two[c, p] + 29
            weights = [
                taps_ref[8 * c + t, count_one + p] for t in range(8)
            ]
            parts = []
            for part in range(2):
                index = (16 * c + beam) * 2 + part
                parts.append(sampled(lambda t: one_taps[t, index], weights, distance, rows_out))
            real, imag = parts
            cosine = turn_two[(2 * i + c) * 2]
            sine = turn_two[(2 * i + c) * 2 + 1]
            turned = (real * cosine - imag * sine, real * sine + imag * cosine)
            for part in range(2):
                sums[part] = turned[part] if c == 0 else sums[part] + turned[part]
        for part in range(2):
            out_ref[2 * i + part] = sums[part].astype(out_ref.dtype)
        return 0

    taps_copy.wait()
    compress(0)
    compress(1)
    first_merges(me // 2)
    compress(2)
    compress(3)
    first_merges(1 - me // 2)
    lax.fori_loop(0, 32, second_merge, 0, unroll=U_TWO)

    for dz in range(GROUP):

        @pl.when(has_left)
        def _():
            copy_to(1, dz).wait_send()

        @pl.when(has_right)
        def _():
            copy_to(2, dz).wait_send()

        if dz:
            copy_to(0, dz).wait_send()


def body(
    echo, chirp, beam_one, shift_one, frac_one, base_one, beam_two, shift_two, frac_two, base_two
):
    beams, _, bins = echo.shape[1:]
    chunks = bins // LANES
    taps = chirp.shape[1]
    fracs = frac_one.shape[1] + frac_two.shape[1]
    arranged = echo[0].reshape(GROUP, 8, 2, chunks, LANES).transpose(0, 3, 2, 1, 4)
    arranged = arranged.reshape(GROUP, chunks, 16, LANES)
    vmem = pl.BlockSpec(memory_space=pltpu.VMEM)
    smem = pl.BlockSpec(memory_space=pltpu.SMEM)
    merged = pl.pallas_call(
        kernel,
        out_shape=jax.ShapeDtypeStruct((beams * 2, chunks, LANES), jnp.bfloat16),
        in_specs=[vmem, pl.BlockSpec(memory_space=pl.ANY)] + [smem] * 8 + [vmem] * 2,
        out_specs=vmem,
        scratch_shapes=[
            pltpu.VMEM((GROUP, LEFT + chunks + RIGHT, 16, LANES), jnp.bfloat16),
            pltpu.VMEM((16, fracs), jnp.float32),
            pltpu.SMEM((16, fracs), jnp.float32),
            pltpu.VMEM((512, 256 + taps), jnp.bfloat16),
            pltpu.VMEM((8 * 2 * 32, LANES), jnp.float32),
            pltpu.VMEM((4, GROUP * 16, 32, LANES), jnp.float32),
            pltpu.VMEM((4, 2 * 16 * 2, 32, LANES), jnp.float32),
            pltpu.VMEM((16 * 2 * 2, 32, LANES), jnp.float32),
            pltpu.VMEM((32 * 2 * 2, chunks, LANES), jnp.float32),
            pltpu.SemaphoreType.DMA((3, GROUP)),
            pltpu.SemaphoreType.DMA((3, GROUP)),
            pltpu.SemaphoreType.DMA,
            pltpu.SemaphoreType.DMA,
        ],
        compiler_params=pltpu.CompilerParams(
            collective_id=0, has_side_effects=True, vmem_limit_bytes=40 * 2**20
        ),
        name="merge_all",
    )(
        chirp, arranged, beam_one, shift_one, frac_one, base_one, beam_two, shift_two, frac_two,
        base_two, frac_one, frac_two,
    )
    return merged.reshape(1, 1, beams, 2, bins)


def solution(mesh):
    in_specs = (
        P(("scene", "pulse"), "rep", None, "range"),
        P(),
        P(),
        P(),
        P(),
        P(),
        P(),
        P(),
        P(),
        P(),
    )
    out_specs = P("rep", ("scene", "pulse"), None, None, "range")
    return jax.shard_map(body, mesh=mesh, in_specs=in_specs, out_specs=out_specs, check_vma=False)
```
